256 devices in a mesh: seq: 32 (over z_lo, y, x), ch: 8 (over z_hi, core).
Axes of the slice: x: 4, y: 4, z: 8 (z_hi: 4, z_lo: 2; z = z_hi * 2 + z_lo), core: 2. Of those that a mesh axis runs over, the one named last changes fastest.
Arguments:
- q_proj: bfloat16 [32768, 4096], P(('seq', 'ch')), may hold values from -6 to 6
- k_proj: bfloat16 [32768, 4096], P(('seq', 'ch')), may hold values from -6 to 6
- v_proj: bfloat16 [32768, 4096], P(('seq', 'ch')), may hold values from -6 to 6
- short_filter: float32 [3, 3, 4096], replicated, may hold values from -3 to 3
- rates: float32 [4096, 16], P('ch'), may hold values from 3.0517578e-05 to 0.03
- residues: float32 [4096, 16], P('ch'), may hold values from -1.5 to 1.5
- skip: float32 [4096], replicated, may hold values from -4 to 4
Outputs:
- mixed: bfloat16 [32768, 4096], P(('seq', 'ch'))
The draws below stay inside these ranges and needn't reach their ends.
All inputs are finite; a program needn't handle non-finite values.
Results may differ from the reference program's by a relative error of at most 0.008.
Values may be sent and summed in bfloat16 or wider, within the bound.
No kernel may reach another device: no remote copies, remote signals or barrier semaphores. Data moves between devices by JAX's collectives and lax.ppermute only.
A program may use at most 192 MiB of HBM per device.

```python
import math
import jax
import jax.numpy as jnp
from jax import lax

D = 4096
MODES = 16
TAPS = 3
TOKENS = 32768


def block_levels(own_key, dims, split, smallest, high):
    level, own = 1.0, jax.random.fold_in(own_key, 6)
    for axis_at, blocks in split:
        heights = jnp.exp(jax.random.uniform(jax.random.fold_in(own, axis_at), (blocks,), jnp.float32, smallest / len(split), high / len(split)))
        level = level * jnp.repeat(heights, dims[axis_at] // blocks).reshape([-1 if axis == axis_at else 1 for axis in range(len(dims))])
    return level


def noise(rng, shape, spread, reach, cuts=(), kind=jnp.bfloat16):
    loudness = block_levels(rng, shape, cuts, -0.22, 0.18) if cuts else 1.0
    array = jax.random.normal(rng, shape, jnp.float32) * spread * loudness
    return jnp.minimum(jnp.maximum(array, -reach), reach).astype(kind)


def setup_inputs(seed: int = 0) -> dict:
    seeds = jax.random.split(jax.random.key(seed), 8)
    return {
        "q_proj": noise(seeds[0], (TOKENS, D), 1.0, 6.0, ((0, 256),)),
        "k_proj": noise(seeds[1], (TOKENS, D), 1.0, 6.0, ((0, 256),)),
        "v_proj": noise(seeds[2], (TOKENS, D), 1.0, 6.0, ((0, 256),)),
        "short_filter": noise(seeds[3], (3, TAPS, D), 0.6, 3.0, (), jnp.float32),
        "rates": jnp.clip(jnp.exp(math.log(0.03) - 6.89065 * jax.random.uniform(seeds[4], (D, MODES), jnp.float32) ** block_levels(seeds[4], (D, MODES), ((0, 8),), -0.2, 0.2)), 3.0517578125e-05, 0.03),
        "residues": noise(seeds[5], (D, MODES), 0.25, 1.5, ((0, 8),), jnp.float32),
        "skip": noise(seeds[6], (D,), 1.0, 4.0, (), jnp.float32),
    }


def widen(value):
    return lax.optimization_barrier(value).astype(jnp.float32)

def short_mix(extended, taps):
    return taps[0] * extended[2:] + taps[1] * extended[1:-1] + taps[2] * extended[:-2]

def padded(values):
    zeros = jnp.zeros((2, values.shape[1]), jnp.float32)
    return jnp.concatenate([zeros, values.astype(jnp.float32)], axis=0)

def filter_values(times, rates, residues):
    weight = residues * jnp.sqrt(-jnp.expm1(-2.0 * rates))

    def add_mode(index, total):
        rate = lax.dynamic_index_in_dim(rates, index, 1, keepdims=False)
        scale = lax.dynamic_index_in_dim(weight, index, 1, keepdims=False)
        return total + scale[None, :] * jnp.exp(-rate[None, :] * times[:, None])
    start = jnp.zeros((times.shape[0], rates.shape[0]), jnp.float32)
    return lax.fori_loop(0, rates.shape[1], add_mode, start)

def reference(q_proj, k_proj, v_proj, short_filter, rates, residues, skip):
    length, width = q_proj.shape
    query = short_mix(padded(q_proj), short_filter[0]).astype(jnp.bfloat16)
    keyed = short_mix(padded(k_proj), short_filter[1])
    valued = short_mix(padded(v_proj), short_filter[2])
    signal = (keyed * valued).astype(jnp.bfloat16)
    block_width = min(width, 256)
    count = width // block_width
    stacked = widen(signal).reshape(length, count, block_width).transpose(1, 0, 2)
    rate_blocks = rates.reshape(count, block_width, rates.shape[1])
    residue_blocks = residues.reshape(count, block_width, residues.shape[1])
    times = jnp.arange(length, dtype=jnp.int32).astype(jnp.float32)

    def convolve(items):
        column, rate_block, residue_block = items
        taps = filter_values(times, rate_block, residue_block)
        spectrum = jnp.fft.rfft(column, n=2 * length, axis=0) * jnp.fft.rfft(taps, n=2 * length, axis=0)
        return jnp.fft.irfft(spectrum, n=2 * length, axis=0)[:length].astype(jnp.float32)
    conv = lax.map(convolve, (stacked, rate_blocks, residue_blocks))
    conv = conv.transpose(1, 0, 2).reshape(length, width).astype(jnp.bfloat16)
    mixed = widen(query) * (widen(conv) + skip[None, :] * widen(signal))
    return mixed.astype(jnp.bfloat16)
```

```python
import functools
import math

import jax
import jax.numpy as jnp
import numpy as np
from jax import lax
from jax.experimental import pallas as pl
from jax.experimental.pallas import tpu as pltpu
from jax.sharding import PartitionSpec as P

F32, BF16 = jnp.float32, jnp.bfloat16
HIGHEST = lax.Precision.HIGHEST
NX, NY, NZ, NH = 4, 4, 2, 4
SPEC = pltpu.PrefetchScalarGridSpec


def transforms(rows):
    k = np.arange(rows)[:, None]
    n = np.arange(rows)[None, :]
    angle = np.pi * (((2 * k + 1) * n) % (4 * rows)) / (2 * rows)
    forward = np.concatenate([np.cos(angle), -np.sin(angle)], axis=0)
    inverse = np.concatenate([np.cos(angle).T, -np.sin(angle).T], axis=1) / rows
    return forward.astype(np.float32), inverse.astype(np.float32)


def rounded(value):
    return value.astype(BF16).astype(F32)


def mix(now, one, two, taps):
    return taps[0:1] * now + taps[1:2] * one + taps[2:3] * two


def mix_block(block, taps):
    return mix(block, pltpu.roll(block, 1, 0), pltpu.roll(block, 2, 0), taps)


def mix_top(block, edge, taps):
    a, b = block[0:1], block[1:2]
    e0, e1 = edge[0:1], edge[1:2]
    return mix(a, e1, e0, taps), mix(b, a, e1, taps)


def signal_kernel(k_ref, v_ref, filt_ref, sig_ref):
    key = mix_block(k_ref[...].astype(F32), filt_ref[1])
    value = mix_block(v_ref[...].astype(F32), filt_ref[2])
    sig_ref[...] = rounded(key * value)


def signal_call(k_proj, v_proj, filt, group):
    rows, width = k_proj.shape
    block = pl.BlockSpec((rows, group), lambda g: (0, g))
    return pl.pallas_call(
        signal_kernel,
        grid=(width // group,),
        in_specs=[block, block, pl.BlockSpec((3, 3, group), lambda g: (0, 0, g))],
        out_specs=block,
        out_shape=jax.ShapeDtypeStruct((rows, width), F32),
        cost_estimate=pl.CostEstimate(flops=rows * width * 12, bytes_accessed=rows * width * 8, transcendentals=0),
    )(k_proj, v_proj, filt)


def lane_group(flip):
    def group(k, place):
        return (place[0] + NH - k) % NH * 2 + (place[1] + flip) % 2

    return group


def state_kernel(place, rate_ref, sig_ref, k_ref, v_ref, edge_ref, filt_ref, state_ref, top_ref):
    rows = sig_ref.shape[0]
    half = rows // 2
    decay = jnp.exp(-rate_ref[0])
    edges = edge_ref[...].astype(F32)
    key = mix_top(k_ref[...].astype(F32), edges[1], filt_ref[1])
    value = mix_top(v_ref[...].astype(F32), edges[2], filt_ref[2])
    s0, s1 = rounded(key[0] * value[0]), rounded(key[1] * value[1])
    row = lax.broadcasted_iota(jnp.int32, top_ref.shape, 0)
    top_ref[...] = jnp.where(row == 0, s0, jnp.where(row == 1, s1, sig_ref[0:8, :]))
    early = s0 * decay + s1
    late = sig_ref[half : half + 1, :] * decay + sig_ref[half + 1 : half + 2, :]
    for t in range(2, half):
        early = early * decay + sig_ref[t : t + 1, :]
        late = late * decay + sig_ref[half + t : half + t + 1, :]
    state_ref[0] = early * jnp.exp(-rate_ref[0] * half) + late


def state_call(place, rates, sig, k_proj, v_proj, edges, filt, flip):
    rows, width = sig.shape
    modes, group = rates.shape[1:]
    at = lane_group(flip)
    return pl.pallas_call(
        state_kernel,
        grid_spec=SPEC(
            num_scalar_prefetch=1,
            grid=(NH,),
            in_specs=[
                pl.BlockSpec((1, modes, group), lambda k, p: (k, 0, 0)),
                pl.BlockSpec((rows, group), lambda k, p: (0, at(k, p))),
                pl.BlockSpec((16, group), lambda k, p: (0, at(k, p))),
                pl.BlockSpec((16, group), lambda k, p: (0, at(k, p))),
                pl.BlockSpec((3, 2, group), lambda k, p: (0, 0, at(k, p))),
                pl.BlockSpec((3, 3, group), lambda k, p: (0, 0, at(k, p))),
            ],
            out_specs=[
                pl.BlockSpec((1, modes, group), lambda k, p: (k, 0, 0)),
                pl.BlockSpec((8, group), lambda k, p: (0, at(k, p))),
            ],
        ),
        out_shape=[
            jax.ShapeDtypeStruct((NH, modes, group), F32),
            jax.ShapeDtypeStruct((rows, width), F32),
        ],
        input_output_aliases={2: 1},
        cost_estimate=pl.CostEstimate(
            flops=rows * width * modes, bytes_accessed=rows * width * 2, transcendentals=0
        ),
    )(place, rates, sig, k_proj, v_proj, edges, filt)


def local_kernel(place, chunk, rate0, rate1, weight0, weight1, sig_ref, q_ref, edge_ref, filt_ref,
                 fwd_ref, inv_ref, _, __, conv_ref, query_ref, taps_ref, rate_s, step_s, weight_s):
    own = (pl.program_id(0) + place[1]) % 2 == 0
    rows, group = sig_ref.shape
    modes = rate_s.shape[0]
    rate_s[...] = jnp.where(own, rate0[0], rate1[0])
    weight_s[...] = jnp.where(own, weight0[0], weight1[0])
    step_s[...] = jnp.exp(-8.0 * rate_s[...])
    ramp = lax.broadcasted_iota(jnp.int32, (8, 128), 0).astype(F32)

    for lane in range(0, group, 128):
        at = slice(lane, lane + 128)
        terms = [
            weight_s[m : m + 1, at] * jnp.exp(-rate_s[m : m + 1, at] * ramp) for m in range(modes)
        ]
        steps = [jnp.broadcast_to(step_s[m : m + 1, at], (8, 128)) for m in range(modes)]
        for tile in range(rows // 8):
            total = functools.reduce(lambda a, b: a + b, terms)
            taps_ref[tile * 8 : tile * 8 + 8, at] = total
            if tile + 1 < rows // 8:
                terms = [a * b for a, b in zip(terms, steps)]

    fwd = fwd_ref[...]
    sig = jnp.dot(fwd, sig_ref[...], precision=HIGHEST, preferred_element_type=F32)
    fil = jnp.dot(fwd, taps_ref[...], precision=HIGHEST, preferred_element_type=F32)
    sr, si, fr, fi = sig[:rows], sig[rows:], fil[:rows], fil[rows:]
    prod = jnp.concatenate([sr * fr - si * fi, sr * fi + si * fr], axis=0)
    conv_ref[...] = jnp.dot(inv_ref[...], prod, precision=HIGHEST, preferred_element_type=F32)

    q = q_ref[...].astype(F32)
    query = mix_block(q, filt_ref[0])
    q0, q1 = mix_top(q, edge_ref[0].astype(F32), filt_ref[0])
    row = lax.broadcasted_iota(jnp.int32, query.shape, 0)
    query_ref[...] = jnp.where(row == 0, q0, jnp.where(row == 1, q1, query)).astype(BF16)


def local_call(place, chunk, rates, weights, sig, q_proj, edges, filt, before):
    rows, width = sig.shape
    modes, group = rates[0].shape[1:]
    fwd, inv = transforms(rows)

    def par(n, p):
        return ((p[0] + NH - chunk) % NH, 0, 0)

    def lanes(n, p):
        return (0, 2 * chunk + n)

    def lanes3(n, p):
        return (0, 0, 2 * chunk + n)

    par_spec = pl.BlockSpec((1, modes, group), par)
    any_spec = pl.BlockSpec(memory_space=pl.ANY)
    body = functools.partial(local_kernel)
    shapes = [jax.ShapeDtypeStruct((rows, width), F32), jax.ShapeDtypeStruct((rows, width), BF16)]

    def kernel(p, r0, r1, w0, w1, s, q, e, f, a, b, *rest):
        if before is None:
            rest = (None, None) + rest
        body(p, chunk, r0, r1, w0, w1, s, q, e, f, a, b, *rest)

    return pl.pallas_call(
        kernel,
        grid_spec=SPEC(
            num_scalar_prefetch=1,
            grid=(2,),
            in_specs=[par_spec] * 4
            + [
                pl.BlockSpec((rows, group), lanes),
                pl.BlockSpec((rows, group), lanes),
                pl.BlockSpec((3, 2, group), lanes3),
                pl.BlockSpec((3, 3, group), lanes3),
                pl.BlockSpec((2 * rows, rows), lambda n, p: (0, 0)),
                pl.BlockSpec((rows, 2 * rows), lambda n, p: (0, 0)),
            ]
            + ([] if before is None else [any_spec, any_spec]),
            out_specs=[pl.BlockSpec((rows, group), lanes), pl.BlockSpec((rows, group), lanes)],
            scratch_shapes=[
                pltpu.VMEM((rows, group), F32),
                pltpu.VMEM((modes, group), F32),
                pltpu.VMEM((modes, group), F32),
                pltpu.VMEM((modes, group), F32),
            ],
        ),
        out_shape=shapes,
        input_output_aliases={} if before is None else {11: 0, 12: 1},
        cost_estimate=pl.CostEstimate(
            flops=rows * width * modes, bytes_accessed=rows * width * 4, transcendentals=0
        ),
    )(place, *rates, *weights, sig, q_proj, edges, filt, jnp.asarray(fwd), jnp.asarray(inv), *(before or ()))


def carry_kernel(place, rate_ref, weight_ref, state_ref, conv_ref, query_ref, sig_ref, skip_ref, *rest):
    out_ref, start_s, step_s, carry_s = rest[-4:]
    rows, group = sig_ref.shape
    modes = rate_ref.shape[1]
    start_s[...] = weight_ref[0] * state_ref[0]
    step_s[...] = jnp.exp(-8.0 * rate_ref[0])
    ramp = lax.broadcasted_iota(jnp.int32, (8, 128), 0).astype(F32) + 1.0
    for lane in range(0, group, 128):
        at = slice(lane, lane + 128)
        terms = [
            start_s[m : m + 1, at] * jnp.exp(-rate_ref[0, m : m + 1, at] * ramp)
            for m in range(modes)
        ]
        steps = [jnp.broadcast_to(step_s[m : m + 1, at], (8, 128)) for m in range(modes)]
        for tile in range(rows // 8):
            total = functools.reduce(lambda a, b: a + b, terms)
            carry_s[tile * 8 : tile * 8 + 8, at] = total
            if tile + 1 < rows // 8:
                terms = [a * b for a, b in zip(terms, steps)]
    conv = rounded(conv_ref[...] + carry_s[...])
    out_ref[...] = (query_ref[...].astype(F32) * (conv + skip_ref[...] * sig_ref[...])).astype(BF16)


def carry_call(place, rates, weights, states, conv, query, sig, skip, flip, before):
    rows, width = sig.shape
    modes, group = rates.shape[1:]
    at = lane_group(flip)
    par = pl.BlockSpec((1, modes, group), lambda k, p: (k, 0, 0))
    block = pl.BlockSpec((rows, group), lambda k, p: (0, at(k, p)))
    return pl.pallas_call(
        carry_kernel,
        grid_spec=SPEC(
            num_scalar_prefetch=1,
            grid=(NH,),
            in_specs=[par, par, par, block, block, block, pl.BlockSpec((1, group), lambda k, p: (0, at(k, p)))]
            + ([] if before is None else [pl.BlockSpec(memory_space=pl.ANY)]),
            out_specs=block,
            scratch_shapes=[
                pltpu.VMEM((modes, group), F32),
                pltpu.VMEM((modes, group), F32),
                pltpu.VMEM((rows, group), F32),
            ],
        ),
        out_shape=jax.ShapeDtypeStruct((rows, width), BF16),
        input_output_aliases={} if before is None else {8: 0},
        cost_estimate=pl.CostEstimate(
            flops=rows * width * modes, bytes_accessed=rows * width * 4, transcendentals=0
        ),
    )(place, rates, weights, states, conv, query, sig, skip, *(() if before is None else (before,)))


def moved(value, axis, target):
    return lax.ppermute(value, axis, [(i, target(i)) for i in range(lax.axis_size(axis))])


def to_chip(value, by):
    return moved(value, "ch", lambda i: (i + 2 * by) % (2 * NH))


def to_core(value):
    return moved(value, "ch", lambda i: i ^ 1)


def to_x(value, by):
    return moved(value, "seq", lambda i: i // NX * NX + (i + by) % NX)


def to_y(value, by):
    span = NX * NY
    return moved(value, "seq", lambda i: i // span * span + (i + by * NX) % span)


def to_z(value):
    return moved(value, "seq", lambda i: (i + NX * NY) % (NX * NY * NZ))


def power(rates, count):
    return jnp.exp(-rates * jnp.asarray(count, F32))


def prefix(values, place, rates, span):
    size = len(values)
    start = jnp.zeros_like(values[0])
    end = jnp.zeros_like(values[0])
    for n, value in enumerate(values):
        source = (place - n) % size
        end += value * power(rates, span * (size - 1 - source))
        if n:
            start += jnp.where(n <= place, value * power(rates, span * (n - 1)), 0.0)
    return start, end


def on_device(q_proj, k_proj, v_proj, short_filter, rates, residues, skip):
    rows, width = q_proj.shape
    seq_at, ch_at = lax.axis_index("seq"), lax.axis_index("ch")
    x_at, y_at, z_at = seq_at % NX, seq_at // NX % NY, seq_at // (NX * NY)
    h_at, core = ch_at // 2, ch_at % 2
    place = jnp.stack([h_at, core]).astype(jnp.int32)
    group = rates.shape[0]

    edges = jnp.stack([q_proj[-2:], k_proj[-2:], v_proj[-2:]])
    total = lax.axis_size(("seq", "ch"))
    edges = lax.ppermute(edges, ("seq", "ch"), [(i, i + 1) for i in range(total - 1)])

    own_rates = rates.T
    rates0 = jnp.stack([own_rates] + [to_chip(own_rates, k) for k in range(1, NH)])
    rates1 = to_core(rates0)
    own_weights = (residues * jnp.sqrt(-jnp.expm1(-2.0 * rates))).T
    weights0 = jnp.stack([own_weights] + [to_chip(own_weights, k) for k in range(1, NH)])
    weights1 = to_core(weights0)

    sig = signal_call(k_proj, v_proj, short_filter, group)
    state0, sig = state_call(place, rates0, sig, k_proj, v_proj, edges, short_filter, 0)
    state1, sig = state_call(place, rates1, sig, k_proj, v_proj, edges, short_filter, 1)

    other1 = to_core(state0)
    first = jnp.where(core == 0, state1, other1)
    second = jnp.where(core == 0, other1, state1)
    chip = first * power(rates1, rows) + second

    mine = rates1[0]
    got = [chip[0]] + [to_chip(chip[k], -k) for k in range(1, NH)]
    whole = jnp.zeros_like(mine)
    starts = [jnp.zeros_like(mine) for _ in range(NH)]
    for k in range(NH):
        source = (h_at + k) % NH
        whole += got[k] * power(mine, 2 * rows * (NH - 1 - source))
        for j in range(NH):
            target = (h_at + j) % NH
            weight = power(mine, 2 * rows * jnp.maximum(target - 1 - source, 0))
            starts[j] += jnp.where(source < target, got[k] * weight, 0.0)

    span = 2 * NH * rows
    before_x, row = prefix([whole] + [to_x(whole, n) for n in range(1, NX)], x_at, mine, span)
    before_y, plane = prefix([row] + [to_y(row, n) for n in range(1, NY)], y_at, mine, span * NX)
    before_z = jnp.where(z_at == 1, to_z(plane), 0.0)
    start = before_x + power(mine, span * x_at) * (
        before_y + power(mine, span * NX * y_at) * before_z
    )
    sent = []
    for j in range(NH):
        target = (h_at + j) % NH
        sent.append(starts[j] + power(mine, 2 * rows * target) * start)
    carry = jnp.stack([sent[0]] + [to_chip(sent[j], j) for j in range(1, NH)])
    later = first + power(rates1, rows) * carry
    carry1 = jnp.where(core == 0, carry, later)
    carry0 = to_core(jnp.where(core == 0, later, carry))

    bufs = None
    for chunk in range(NH):
        bufs = local_call(
            place, chunk, (rates0, rates1), (weights0, weights1), sig, q_proj, edges, short_filter, bufs
        )
    conv, query = bufs

    skip = skip[None, :]
    out = carry_call(place, rates1, weights1, carry1, conv, query, sig, skip, 1, None)
    return carry_call(place, rates0, weights0, carry0, conv, query, sig, skip, 0, out)


def solution(mesh):
    placed = (
        P(("seq", "ch"), None),
        P(("seq", "ch"), None),
        P(("seq", "ch"), None),
        P(),
        P("ch", None),
        P("ch", None),
        P(),
    )
    return jax.shard_map(
        on_device, mesh=mesh, in_specs=placed, out_specs=P(("seq", "ch"), None), check_vma=False
    )
```

```python
import functools

import jax
import jax.numpy as jnp
import numpy as np
from jax import lax
from jax.experimental import pallas as pl
from jax.experimental.pallas import tpu as pltpu
from jax.sharding import PartitionSpec as P

F32, BF16 = jnp.float32, jnp.bfloat16
NH = 4
LANE = 128
VMEM = pl.BlockSpec(memory_space=pltpu.VMEM)
ANY = pl.BlockSpec(memory_space=pl.ANY)
HBM = pl.BlockSpec(memory_space=pltpu.HBM)
GRANT = pltpu.CompilerParams(vmem_limit_bytes=60 << 20)


def two_parts(value):
    high = value.astype(BF16)
    return high, (value - high.astype(F32)).astype(BF16)


def transforms(rows):
    k = np.arange(rows)[:, None]
    n = np.arange(rows)[None, :]
    angle = np.pi * (((2 * k + 1) * n) % (4 * rows)) / (2 * rows)
    forward = np.concatenate([np.cos(angle), -np.sin(angle)], axis=0).astype(np.float32)
    inverse = (np.concatenate([np.cos(angle).T, -np.sin(angle).T], axis=1) / rows).astype(np.float32)
    bf16 = jnp.bfloat16

    def parts(array):
        high = array.astype(bf16)
        return high, (array - high.astype(np.float32)).astype(bf16)

    fh, fl = parts(forward)
    gh, gl = parts(inverse)
    return np.concatenate([fh, fl, fh], axis=1), np.concatenate([gh, gl, gh], axis=1)


def rounded(value):
    return value.astype(BF16).astype(F32)


def mix(now, one, two, taps):
    return taps[0:1] * now + taps[1:2] * one + taps[2:3] * two


def mix_top(block, edge, taps):
    a, b = block[0:1], block[1:2]
    e0, e1 = edge[0:1], edge[1:2]
    return mix(a, e1, e0, taps), mix(b, a, e1, taps)


def top_rows(first, second, rest):
    row = lax.broadcasted_iota(jnp.int32, rest.shape, 0)
    return jnp.where(row == 0, first, jnp.where(row == 1, second, rest))


def shifts(rows):
    return np.concatenate([np.roll(np.eye(rows), n, axis=0) for n in range(3)], axis=0).astype(jnp.bfloat16)


def mix_shifted(shift, block, taps):
    rows = block.shape[0]
    parts = jnp.dot(shift, block, preferred_element_type=F32)
    return mix(parts[:rows], parts[rows : 2 * rows], parts[2 * rows :], taps)


def edge_kernel(q_ref, k_ref, v_ref, edge_ref, last, sems):
    mover = Mover(sems)
    rows = q_ref.shape[0]
    copies = [
        mover.start(ref.at[rows - 16 : rows], last.at[n]) for n, ref in enumerate((q_ref, k_ref, v_ref))
    ]
    for copy in copies:
        copy.wait()
    for at in range(0, edge_ref.shape[1], 512):
        lanes = slice(at, at + 512)
        two = [last[n, :, lanes].astype(F32)[14:] for n in range(3)]
        edge_ref[:, lanes] = jnp.concatenate(two + [two[0]], axis=0)


def edge_call(q_proj, k_proj, v_proj):
    width = q_proj.shape[1]
    return pl.pallas_call(
        edge_kernel,
        in_specs=[ANY, ANY, ANY],
        out_specs=VMEM,
        out_shape=jax.ShapeDtypeStruct((8, width), F32),
        scratch_shapes=[pltpu.VMEM((3, 16, width), BF16), pltpu.SemaphoreType.DMA((3,))],
        compiler_params=GRANT,
        cost_estimate=cost(1 << 20),
    )(q_proj, k_proj, v_proj)


def signal_kernel(k_any, v_any, filt_any, sig_any, k, v, filt, line, sig, sems):
    mover = Mover(sems)
    rows, width = k.shape
    group = 512
    parts = [slice(at, at + group) for at in range(0, width, group)]
    small = [mover.start(filt_any.at[1:3], filt)]
    fetched = [
        (mover.start(k_any.at[:, at], k.at[:, at]), mover.start(v_any.at[:, at], v.at[:, at])) for at in parts
    ]
    for copy in small:
        copy.wait()
    line[:, 0:8, :] = jnp.zeros((4, 8, LANE), F32)

    def short(array, taps, slot, here):
        line[slot, 8:, :] = array[:, here].astype(F32)
        return mix(line[slot, 8:, :], line[slot, 7 : rows + 7, :], line[slot, 6 : rows + 6, :], taps)

    sent = []
    for at, copies in zip(parts, fetched):
        for copy in copies:
            copy.wait()
        for lane in range(at.start, at.stop, LANE):
            here = slice(lane, lane + LANE)
            slot = lane // LANE % 2 * 2
            key = short(k, filt[0, :, here], slot, here)
            value = short(v, filt[1, :, here], slot + 1, here)
            sig[:, here] = (key * value).astype(BF16)
        sent.append(mover.start(sig.at[:, at], sig_any.at[:, at]))
    for copy in sent:
        copy.wait()


def signal_call(k_proj, v_proj, filt):
    rows, width = k_proj.shape
    whole = ((rows, width), BF16)
    return run(
        signal_kernel,
        k_proj, v_proj, filt,
        out=[whole],
        scratch=[whole, whole, ((2, 3, width), F32), ((4, rows + 8, LANE), F32), whole],
        copies=1 + 3 * (width // 512),
        flops=rows * width * 12,
    )[0]


def where_am_i():
    ch = lax.axis_index("ch")
    return ch // 2, lax.rem(ch, 2), lax.axis_index("seq") * 2 * NH + ch


def cost(flops):
    return pl.CostEstimate(flops=flops, bytes_accessed=1 << 20, transcendentals=0)


def run(kernel, *operands, out, scratch=(), copies=1, flops=1 << 20, near=(), near_out=()):
    operands = [
        pltpu.with_memory_space_constraint(value, pltpu.VMEM if n in near else pltpu.HBM)
        for n, value in enumerate(operands)
    ]
    return pl.pallas_call(
        kernel,
        in_specs=[VMEM if n in near else HBM for n in range(len(operands))],
        out_specs=[VMEM if n in near_out else HBM for n in range(len(out))],
        out_shape=[
            pltpu.VMEM(*shape) if n in near_out else pltpu.HBM(*shape)
            for n, shape in enumerate(out)
        ],
        scratch_shapes=[*[pltpu.VMEM(*shape) for shape in scratch], pltpu.SemaphoreType.DMA((copies,))],
        compiler_params=pltpu.CompilerParams(vmem_limit_bytes=(24 if near or near_out else 60) << 20),
        cost_estimate=cost(flops),
    )(*operands)


class Mover:
    def __init__(self, sems):
        self.sems, self.used = sems, 0

    def start(self, source, target):
        copy = pltpu.make_async_copy(source, target, self.sems.at[self.used])
        self.used += 1
        copy.start()
        return copy


def param_at(place, chip):
    return lax.rem(place[0] + NH - chip, NH)


def params_of(place, chip, parity, par0, par1, rows):
    which = param_at(place, chip)
    return jnp.where(place[1] == parity, par0[which, rows, :], par1[which, rows, :])


def weights_of(rates, residues):
    gap = -2.0 * rates
    series = 1.0 + gap * (0.5 + gap * (1 / 6 + gap * (1 / 24 + gap * (1 / 120 + gap * (1 / 720)))))
    return residues * jnp.sqrt(-jnp.where(gap > -0.1, gap * series, jnp.exp(gap) - 1.0))


def fetch_params(mover, arrays, par0, par1):
    return [
        mover.start(array, (par0, par1)[n // NH].at[n % NH]) for n, array in enumerate(arrays)
    ]


def states(rates, first, second, sig_ref, at):
    rows = sig_ref.shape[0]
    half = rows // 2
    decay = jnp.exp(-rates)
    early = first * decay + second
    late = sig_ref[half : half + 1, at] * decay + sig_ref[half + 1 : half + 2, at]
    for t in range(2, half):
        early = early * decay + sig_ref[t : t + 1, at]
        late = late * decay + sig_ref[half + t : half + t + 1, at]
    return early * jnp.exp(-rates * half) + late


def own_decay(place, par0, par1, span):
    modes, group = par0.shape[1] // 2, par0.shape[2]
    per_group = modes * group // (2 * LANE)
    mine = place[2]
    chip, parity = mine // (2 * per_group), lax.rem(mine // per_group, 2)
    mode, part = lax.rem(mine, per_group) // 2, lax.rem(mine, 2)
    at = pl.ds(pl.multiple_of(part * (group // 2), group // 2), group // 2)
    which = param_at(place, chip)
    rate = jnp.where(
        parity == place[1], par0[which, pl.ds(mode, 1), at], par1[which, pl.ds(mode, 1), at]
    )
    row = lax.broadcasted_iota(jnp.int32, (8, LANE), 0)
    return jnp.exp(-span * jnp.where(lax.rem(row, 2) == 0, rate[:, :LANE], rate[:, LANE:]))


def state_kernel(*refs):
    pars, (sig_any, k_any, v_any, edge, filt_any, state, top_any, decay) = refs[: 2 * NH], refs[2 * NH : 2 * NH + 8]
    par0, par1, packed, k_top, v_top, filt, sig, top, sems = refs[2 * NH + 8 :]
    place = where_am_i()
    mover = Mover(sems)
    modes, group = par0.shape[1] // 2, par0.shape[2]
    width = top.shape[1]
    blocks = group // LANE
    small = [
        mover.start(filt_any.at[1:3], filt),
        mover.start(k_any.at[0:16], k_top),
        mover.start(v_any.at[0:16], v_top),
    ]
    for n, array in enumerate(pars):
        (par0, par1)[n // NH][n % NH] = array[...]
    parts = [slice(at, at + group) for at in range(0, width, group)]
    signals = [mover.start(sig_any.at[:, at], packed.at[:, at]) for at in parts]
    for copy in small:
        copy.wait()
    for n, at in enumerate(parts):
        signals[n].wait()
        sig[...] = packed[:, at].astype(F32)
        key = mix_top(k_top[:, at].astype(F32), edge[2:4, at], filt[0, :, at])
        value = mix_top(v_top[:, at].astype(F32), edge[4:6, at], filt[1, :, at])
        s0, s1 = rounded(key[0] * value[0]), rounded(key[1] * value[1])
        top[:, at] = top_rows(s0, s1, sig[0:16, :]).astype(BF16)
        rates = params_of(place, n // 2, n % 2, par0, par1, slice(0, modes))
        value = states(rates, s0, s1, sig, slice(0, group))
        base = n * modes * blocks
        for j in range(blocks):
            state[pl.ds(base + j, modes, stride=blocks), :] = value[:, j * LANE : (j + 1) * LANE]
    sent = mover.start(top, top_any)
    decay[...] = own_decay(place, par0, par1, float(sig.shape[0]))
    sent.wait()


def state_call(pars, sig, k_proj, v_proj, edges, filt):
    rows, width = k_proj.shape
    modes, group = pars[0].shape[0] // 2, pars[0].shape[1]
    par = ((NH, 2 * modes, group), F32)
    count = modes * width // LANE
    return run(
        state_kernel,
        *pars, sig, k_proj, v_proj, edges, filt,
        out=[((count, LANE), F32), ((16, width), BF16), ((8, LANE), F32)],
        scratch=[
            par, par, ((rows, width), BF16), ((16, width), BF16), ((16, width), BF16),
            ((2, 3, width), F32), ((rows, group), F32), ((16, width), BF16),
        ],
        near=[*range(2 * NH), 2 * NH + 3],
        near_out=[0, 2],
        copies=4 + width // group,
        flops=rows * width * modes * 2,
    )


def scan_kernel(got_ref, decay_ref, out_ref, _):
    decay = decay_ref[0:2, :]
    total = jnp.zeros((2, LANE), F32)
    for n in range(got_ref.shape[0]):
        out_ref[n] = total
        total = total * decay + got_ref[n]


def scan_call(got, decay):
    return run(scan_kernel, got, decay, out=[(got.shape, F32)], near=[0, 1], near_out=[0], flops=got.size * 2)[0]


def decaying_sum(start_ref, rate_ref, step_ref, at, first, store, rows):
    modes = start_ref.shape[0]
    ramp = lax.broadcasted_iota(jnp.int32, (8, LANE), 0).astype(F32) + first
    terms = [start_ref[m : m + 1, at] * jnp.exp(-rate_ref[m : m + 1, at] * ramp) for m in range(modes)]
    steps = [jnp.broadcast_to(step_ref[m : m + 1, at], (8, LANE)) for m in range(modes)]
    for tile in range(rows // 8):
        total = terms
        while len(total) > 1:
            total = [a + b for a, b in zip(total[::2], total[1::2])]
        store(slice(tile * 8, tile * 8 + 8), total[0])
        if tile + 1 < rows // 8:
            terms = [a * b for a, b in zip(terms, steps)]


def local_kernel(first, *refs):
    sig_ref, top_ref, q_ref, edge_ref, filt_ref, fwd_ref, inv_ref, shift_ref, conv_ref, query_ref = refs[2 * NH : 2 * NH + 10]
    par0, par1, taps_ref, rate_s, step_s, weight_s, sems = refs[2 * NH + 10 :]
    place = where_am_i()
    rows, group = sig_ref.shape
    modes = par0.shape[1] // 2
    step = pl.program_id(0) + first
    chip, parity = step // 2, lax.rem(step, 2)

    @pl.when(pl.program_id(0) == 0)
    def _():
        for copy in fetch_params(Mover(sems), refs[: 2 * NH], par0, par1):
            copy.wait()

    rate_s[...] = params_of(place, chip, parity, par0, par1, slice(0, modes))
    weight_s[...] = weights_of(
        rate_s[...], params_of(place, chip, parity, par0, par1, slice(modes, 2 * modes))
    )
    step_s[...] = jnp.exp(-8.0 * rate_s[...])

    def body(n, _):
        lanes = pl.ds(pl.multiple_of(n * LANE, LANE), LANE)

        def store(tile, value):
            taps_ref[tile, lanes] = value

        decaying_sum(weight_s, rate_s, step_s, lanes, 0.0, store, rows)
        return 0

    lax.fori_loop(0, group // LANE, body, 0)
    x = jnp.concatenate([top_ref[...], sig_ref[16:, :]], axis=0)
    th, tl = two_parts(taps_ref[...])
    sig = jnp.dot(fwd_ref[:, : 2 * rows], jnp.concatenate([x, x], axis=0), preferred_element_type=F32)
    fil = jnp.dot(fwd_ref[...], jnp.concatenate([th, th, tl], axis=0), preferred_element_type=F32)
    sr, si, fr, fi = sig[:rows], sig[rows:], fil[:rows], fil[rows:]
    ph, pw = two_parts(jnp.concatenate([sr * fr - si * fi, sr * fi + si * fr], axis=0))
    conv_ref[...] = jnp.dot(
        inv_ref[...], jnp.concatenate([ph, ph, pw], axis=0), preferred_element_type=F32
    )
    query = mix_shifted(shift_ref[...], q_ref[...], filt_ref[0])
    q0, q1 = mix_top(q_ref[0:16, :].astype(F32), edge_ref[0:2, :], filt_ref[0])
    query_ref[...] = top_rows(q0, q1, query).astype(BF16)


def local_call(half, pars, sig, top, q_proj, edges, filt, fwd, inv, shift):
    rows, width = q_proj.shape
    modes, group = pars[0].shape[0] // 2, pars[0].shape[1]
    par = pltpu.VMEM((NH, 2 * modes, group), F32)
    first = half * NH

    def lanes(n):
        return (0, n + first)

    def whole(array):
        return pl.BlockSpec(array.shape, lambda n: (0,) * array.ndim)

    block = pl.BlockSpec((rows, group), lambda n: (0, n))
    return pl.pallas_call(
        functools.partial(local_kernel, first),
        grid=(NH,),
        in_specs=[ANY] * (2 * NH) + [
            pl.BlockSpec((rows, group), lanes), pl.BlockSpec((16, group), lanes), pl.BlockSpec((rows, group), lanes),
            pl.BlockSpec((8, group), lanes), pl.BlockSpec((3, 3, group), lambda n: (0, 0, n + first)),
            whole(fwd), whole(inv), whole(shift),
        ],
        out_specs=[block, block],
        out_shape=[
            jax.ShapeDtypeStruct((rows, width // 2), F32),
            jax.ShapeDtypeStruct((rows, width // 2), BF16),
        ],
        scratch_shapes=[par, par, pltpu.VMEM((rows, group), F32)]
        + [pltpu.VMEM((modes, group), F32)] * 3 + [pltpu.SemaphoreType.DMA((2 * NH,))],
        compiler_params=GRANT,
        cost_estimate=cost(rows * rows * group * 16 * NH),
    )(*pars, sig, top, q_proj, edges, filt, fwd, inv, shift)


def carry_kernel(*refs):
    pars, (state, top_any, skip_any, sig_any) = refs[: 2 * NH], refs[2 * NH : 2 * NH + 4]
    conv_anys, query_anys = refs[2 * NH + 4 : 2 * NH + 6], refs[2 * NH + 6 : 2 * NH + 8]
    out_any, par0, par1, sig, top, skip, conv, query, out, start_s, step_s, rate_s, sems = refs[2 * NH + 8 :]
    place = where_am_i()
    mover = Mover(sems)
    rows, width = sig.shape
    modes, group = par0.shape[1] // 2, par0.shape[2]
    blocks = group // LANE
    small = [
        *fetch_params(mover, pars, par0, par1),
        mover.start(top_any, top),
        mover.start(skip_any, skip),
    ]
    span = width // 2
    parts = [slice(at, at + group) for at in range(0, width, group)]
    fetched = []
    for at in parts:
        n, inside = at.start // span, slice(at.start % span, at.start % span + group)
        fetched.append(
            [
                mover.start(conv_anys[n].at[:, inside], conv.at[:, at]),
                mover.start(query_anys[n].at[:, inside], query.at[:, at]),
                mover.start(sig_any.at[:, at], sig.at[:, at]),
            ]
        )
    for copy in small:
        copy.wait()
    sent = []
    for n, at in enumerate(parts):
        rate_s[...] = params_of(place, n // 2, n % 2, par0, par1, slice(0, modes))
        step_s[...] = jnp.exp(-8.0 * rate_s[...])
        weights = weights_of(
            rate_s[...], params_of(place, n // 2, n % 2, par0, par1, slice(modes, 2 * modes))
        )
        for j in range(blocks):
            lanes = slice(j * LANE, (j + 1) * LANE)
            from_state = state[pl.ds(n * modes * blocks + j, modes, stride=blocks), :]
            start_s[:, lanes] = weights[:, lanes] * from_state
        for copy in fetched[n]:
            copy.wait()

        def body(j, _):
            lanes = pl.ds(pl.multiple_of(j * LANE, LANE), LANE)
            here = pl.ds(pl.multiple_of(at.start + j * LANE, LANE), LANE)
            direct = skip[:, here]
            held = []

            def store(tile, value):
                held.append(rounded(conv[tile, here] + value))
                if len(held) == 2:
                    both = slice(tile.start - 8, tile.stop)
                    signal = (top[:, here] if both.start == 0 else sig[both, here]).astype(F32)
                    total = jnp.concatenate(held, axis=0) + direct * signal
                    out[both, here] = (query[both, here].astype(F32) * total).astype(BF16)
                    held.clear()

            decaying_sum(start_s, rate_s, step_s, lanes, 1.0, store, rows)
            return 0

        lax.fori_loop(0, blocks, body, 0)
        sent.append(mover.start(out.at[:, at], out_any.at[:, at]))
    for copy in sent:
        copy.wait()


def carry_call(pars, states, top, skip, sig, convs, queries):
    rows, width = sig.shape
    modes, group = pars[0].shape[0] // 2, pars[0].shape[1]
    par, half = ((NH, 2 * modes, group), F32), ((rows, width), BF16)
    return run(
        carry_kernel,
        *pars, states, top, skip, sig, *convs, *queries,
        out=[half],
        scratch=[
            par, par, half, (top.shape, BF16), (skip.shape, F32),
            ((rows, width), F32), half, half,
        ] + [((modes, group), F32)] * 3,
        near=[2 * NH],
        copies=2 + 2 * NH + 4 * (width // group),
        flops=rows * width * modes * 2,
    )[0]


def moved(value, target):
    return lax.ppermute(value, "ch", [(i, target(i)) for i in range(2 * NH)])


def to_chip(value, by):
    return moved(value, lambda i: (i + 2 * by) % (2 * NH))


def to_core(value):
    return moved(value, lambda i: i ^ 1)


def after(value, *others):
    return lax.optimization_barrier((value, *others))[0]


def on_device(q_proj, k_proj, v_proj, short_filter, rates, residues, skip):
    rows, width = q_proj.shape
    everyone = ("seq", "ch")
    total = lax.axis_size(everyone)
    fwd, inv = (jnp.asarray(a) for a in transforms(rows))
    shift = jnp.asarray(shifts(rows))

    own = jnp.concatenate([rates.T, residues.T], axis=0)
    far = to_chip(own, 2)
    edges = edge_call(q_proj, k_proj, v_proj)
    one = to_chip(after(own, edges), 1)
    edges = lax.ppermute(edges, everyone, [(i, i + 1) for i in range(total - 1)])
    three = to_chip(own, 3)
    sig = signal_call(k_proj, v_proj, short_filter)
    mine = [own, one, far, three]
    pars = mine + [to_core(own)] + [to_core(after(value, sig)) for value in mine[1:]]
    states, top, decay = state_call(pars, sig, k_proj, v_proj, edges, short_filter)

    def exchange(value):
        return lax.all_to_all(value, everyone, 0, 0, tiled=True)

    def local(half):
        return local_call(half, pars, sig, top, q_proj, edges, short_filter, fwd, inv, shift)

    got = exchange(states.reshape(total, -1, LANE))
    got, *early = lax.optimization_barrier((got, *local(0)))
    carry = exchange(scan_call(got, decay))
    carry, *late = lax.optimization_barrier((carry, *local(1)))
    convs, queries = zip(early, late)
    return carry_call(pars, carry.reshape(states.shape), top, skip[None, :], sig, convs, queries)


def solution(mesh):
    placed = (
        P(("seq", "ch"), None),
        P(("seq", "ch"), None),
        P(("seq", "ch"), None),
        P(),
        P("ch", None),
        P("ch", None),
        P(),
    )
    return jax.shard_map(
        on_device, mesh=mesh, in_specs=placed, out_specs=P(("seq", "ch"), None), check_vma=False
    )
```

```python
import functools

import jax
import jax.numpy as jnp
import numpy as np
from jax import lax
from jax.experimental import pallas as pl
from jax.experimental.pallas import tpu as pltpu
from jax.sharding import PartitionSpec as P

F32, BF16 = jnp.float32, jnp.bfloat16
NH = 4
LANE = 128
VMEM = pl.BlockSpec(memory_space=pltpu.VMEM)
ANY = pl.BlockSpec(memory_space=pl.ANY)
HBM = pl.BlockSpec(memory_space=pltpu.HBM)
GRANT = pltpu.CompilerParams(vmem_limit_bytes=60 << 20)


def two_parts(value):
    high = value.astype(BF16)
    return high, (value - high.astype(F32)).astype(BF16)


def transforms(rows):
    k = np.arange(rows)[:, None]
    n = np.arange(rows)[None, :]
    angle = np.pi * (((2 * k + 1) * n) % (4 * rows)) / (2 * rows)
    forward = np.concatenate([np.cos(angle), -np.sin(angle)], axis=0).astype(np.float32)
    inverse = (np.concatenate([np.cos(angle).T, -np.sin(angle).T], axis=1) / rows).astype(np.float32)
    bf16 = jnp.bfloat16

    def parts(array):
        high = array.astype(bf16)
        return high, (array - high.astype(np.float32)).astype(bf16)

    fh, fl = parts(forward)
    gh, gl = parts(inverse)
    return np.concatenate([fh, fl, fh], axis=1), np.concatenate([gh, gl, gh], axis=1)


def rounded(value):
    return value.astype(BF16).astype(F32)


def mix(now, one, two, taps):
    return taps[0:1] * now + taps[1:2] * one + taps[2:3] * two


def mix_top(block, edge, taps):
    a, b = block[0:1], block[1:2]
    e0, e1 = edge[0:1], edge[1:2]
    return mix(a, e1, e0, taps), mix(b, a, e1, taps)


def top_rows(first, second, rest):
    row = lax.broadcasted_iota(jnp.int32, rest.shape, 0)
    return jnp.where(row == 0, first, jnp.where(row == 1, second, rest))


def shifts(rows):
    return np.concatenate([np.roll(np.eye(rows), n, axis=0) for n in range(3)], axis=0).astype(jnp.bfloat16)


def mix_shifted(shift, block, taps):
    rows = block.shape[0]
    parts = jnp.dot(shift, block, preferred_element_type=F32)
    return mix(parts[:rows], parts[rows : 2 * rows], parts[2 * rows :], taps)


def edge_kernel(q_ref, k_ref, v_ref, edge_ref, last, sems):
    mover = Mover(sems)
    rows = q_ref.shape[0]
    copies = [
        mover.start(ref.at[rows - 16 : rows], last.at[n]) for n, ref in enumerate((q_ref, k_ref, v_ref))
    ]
    for copy in copies:
        copy.wait()
    for n in range(3):
        edge_ref[n] = last[n, 14:16, :]


def edge_call(q_proj, k_proj, v_proj):
    width = q_proj.shape[1]
    return pl.pallas_call(
        edge_kernel,
        in_specs=[ANY, ANY, ANY],
        out_specs=VMEM,
        out_shape=jax.ShapeDtypeStruct((3, 2, width), BF16),
        scratch_shapes=[pltpu.VMEM((3, 16, width), BF16), pltpu.SemaphoreType.DMA((3,))],
        compiler_params=GRANT,
        cost_estimate=cost(1 << 20),
    )(q_proj, k_proj, v_proj)


def signal_kernel(k_any, v_any, filt_any, sig_any, k, v, filt, line, sig, sems):
    mover = Mover(sems)
    rows, width = k.shape
    group = 512
    parts = [slice(at, at + group) for at in range(0, width, group)]
    small = [mover.start(filt_any.at[1:3], filt)]
    fetched = [
        (mover.start(k_any.at[:, at], k.at[:, at]), mover.start(v_any.at[:, at], v.at[:, at])) for at in parts
    ]
    for copy in small:
        copy.wait()
    line[:, 0:8, :] = jnp.zeros((4, 8, LANE), F32)

    def short(array, taps, slot, here):
        line[slot, 8:, :] = array[:, here].astype(F32)
        return mix(line[slot, 8:, :], line[slot, 7 : rows + 7, :], line[slot, 6 : rows + 6, :], taps)

    sent = []
    for at, copies in zip(parts, fetched):
        for copy in copies:
            copy.wait()
        for lane in range(at.start, at.stop, LANE):
            here = slice(lane, lane + LANE)
            slot = lane // LANE % 2 * 2
            key = short(k, filt[0, :, here], slot, here)
            value = short(v, filt[1, :, here], slot + 1, here)
            sig[:, here] = (key * value).astype(BF16)
        sent.append(mover.start(sig.at[:, at], sig_any.at[:, at]))
    for copy in sent:
        copy.wait()


def signal_call(k_proj, v_proj, filt):
    rows, width = k_proj.shape
    whole = ((rows, width), BF16)
    return run(
        signal_kernel,
        k_proj, v_proj, filt,
        out=[whole],
        scratch=[whole, whole, ((2, 3, width), F32), ((4, rows + 8, LANE), F32), whole],
        copies=1 + 3 * (width // 512),
        flops=rows * width * 12,
    )[0]


def where_am_i():
    ch = lax.axis_index("ch")
    return ch // 2, lax.rem(ch, 2), lax.axis_index("seq") * 2 * NH + ch


def cost(flops):
    return pl.CostEstimate(flops=flops, bytes_accessed=1 << 20, transcendentals=0)


def run(kernel, *operands, out, scratch=(), copies=1, flops=1 << 20, near=(), near_out=()):
    operands = [
        pltpu.with_memory_space_constraint(value, pltpu.VMEM if n in near else pltpu.HBM)
        for n, value in enumerate(operands)
    ]
    return pl.pallas_call(
        kernel,
        in_specs=[VMEM if n in near else HBM for n in range(len(operands))],
        out_specs=[VMEM if n in near_out else HBM for n in range(len(out))],
        out_shape=[
            pltpu.VMEM(*shape) if n in near_out else pltpu.HBM(*shape)
            for n, shape in enumerate(out)
        ],
        scratch_shapes=[*[pltpu.VMEM(*shape) for shape in scratch], pltpu.SemaphoreType.DMA((copies,))],
        compiler_params=pltpu.CompilerParams(vmem_limit_bytes=(24 if near or near_out else 60) << 20),
        cost_estimate=cost(flops),
    )(*operands)


class Mover:
    def __init__(self, sems):
        self.sems, self.used = sems, 0

    def start(self, source, target):
        copy = pltpu.make_async_copy(source, target, self.sems.at[self.used])
        self.used += 1
        copy.start()
        return copy


def param_at(place, chip):
    return lax.rem(place[0] + NH - chip, NH)


def params_of(place, chip, parity, par0, par1, rows):
    which = param_at(place, chip)
    return jnp.where(place[1] == parity, par0[which, rows, :], par1[which, rows, :])


def weights_of(rates, residues):
    gap = -2.0 * rates
    series = 1.0 + gap * (0.5 + gap * (1 / 6 + gap * (1 / 24 + gap * (1 / 120 + gap * (1 / 720)))))
    return residues * jnp.sqrt(-jnp.where(gap > -0.1, gap * series, jnp.exp(gap) - 1.0))


def fetch_params(mover, arrays, par0, par1):
    return [
        mover.start(array, (par0, par1)[n // NH].at[n % NH]) for n, array in enumerate(arrays)
    ]


def states(rates, first, second, sig_ref, at):
    rows = sig_ref.shape[0]
    half = rows // 2
    decay = jnp.exp(-rates)
    early = first * decay + second
    late = sig_ref[half : half + 1, at] * decay + sig_ref[half + 1 : half + 2, at]
    for t in range(2, half):
        early = early * decay + sig_ref[t : t + 1, at]
        late = late * decay + sig_ref[half + t : half + t + 1, at]
    return early * jnp.exp(-rates * half) + late


def own_decay(place, par0, par1, span):
    modes, group = par0.shape[1] // 2, par0.shape[2]
    per_group = modes * group // (2 * LANE)
    mine = place[2]
    chip, parity = mine // (2 * per_group), lax.rem(mine // per_group, 2)
    mode, part = lax.rem(mine, per_group) // 2, lax.rem(mine, 2)
    at = pl.ds(pl.multiple_of(part * (group // 2), group // 2), group // 2)
    which = param_at(place, chip)
    rate = jnp.where(
        parity == place[1], par0[which, pl.ds(mode, 1), at], par1[which, pl.ds(mode, 1), at]
    )
    row = lax.broadcasted_iota(jnp.int32, (8, LANE), 0)
    return jnp.exp(-span * jnp.where(lax.rem(row, 2) == 0, rate[:, :LANE], rate[:, LANE:]))


def state_kernel(*refs):
    pars, (sig_any, k_any, v_any, edge, filt_any, state_out, top_any, decay, edge_any) = refs[: 2 * NH], refs[2 * NH : 2 * NH + 9]
    par0, par1, packed, k_top, v_top, filt, sig, top, state, sems = refs[2 * NH + 9 :]
    place = where_am_i()
    mover = Mover(sems)
    modes, group = par0.shape[1] // 2, par0.shape[2]
    width = top.shape[1]
    blocks = group // LANE
    small = [
        mover.start(filt_any.at[1:3], filt),
        mover.start(k_any.at[0:16], k_top),
        mover.start(v_any.at[0:16], v_top),
    ]
    for n, array in enumerate(pars):
        (par0, par1)[n // NH][n % NH] = array[...]
    parts = [slice(at, at + group) for at in range(0, width, group)]
    signals = [mover.start(sig_any.at[:, at], packed.at[:, at]) for at in parts]
    kept = mover.start(edge, edge_any)
    for copy in small:
        copy.wait()
    for n, at in enumerate(parts):
        signals[n].wait()
        sig[...] = packed[:, at].astype(F32)
        key = mix_top(k_top[:, at].astype(F32), edge[1, :, at].astype(F32), filt[0, :, at])
        value = mix_top(v_top[:, at].astype(F32), edge[2, :, at].astype(F32), filt[1, :, at])
        s0, s1 = rounded(key[0] * value[0]), rounded(key[1] * value[1])
        top[:, at] = top_rows(s0, s1, sig[0:16, :]).astype(BF16)
        rates = params_of(place, n // 2, n % 2, par0, par1, slice(0, modes))
        value = states(rates, s0, s1, sig, slice(0, group))
        base = n * modes * blocks
        for j in range(blocks):
            state[pl.ds(base + j, modes, stride=blocks), :] = value[:, j * LANE : (j + 1) * LANE]
    sent = mover.start(top, top_any)
    decay[...] = own_decay(place, par0, par1, float(sig.shape[0]))
    state_out[...] = state[...].astype(BF16)
    sent.wait()
    kept.wait()


def state_call(pars, sig, k_proj, v_proj, edges, filt):
    rows, width = k_proj.shape
    modes, group = pars[0].shape[0] // 2, pars[0].shape[1]
    par = ((NH, 2 * modes, group), F32)
    count = modes * width // LANE
    return run(
        state_kernel,
        *pars, sig, k_proj, v_proj, edges, filt,
        out=[((count, LANE), BF16), ((16, width), BF16), ((8, LANE), F32), (edges.shape, BF16)],
        scratch=[
            par, par, ((rows, width), BF16), ((16, width), BF16), ((16, width), BF16),
            ((2, 3, width), F32), ((rows, group), F32), ((16, width), BF16), ((count, LANE), F32),
        ],
        near=[*range(2 * NH), 2 * NH + 3],
        near_out=[0, 2],
        copies=5 + width // group,
        flops=rows * width * modes * 2,
    )


def scan_kernel(got_ref, decay_ref, out_ref, got, sent, _):
    got[...] = got_ref[...].astype(F32)
    decay = decay_ref[0:2, :]
    total = jnp.zeros((2, LANE), F32)
    for n in range(0, got.shape[0], 2):
        sent[n : n + 2, :] = total
        total = total * decay + got[n : n + 2, :]
    out_ref[...] = sent[...].astype(BF16)


def scan_call(got, decay):
    return run(
        scan_kernel, got, decay,
        out=[(got.shape, BF16)], scratch=[(got.shape, F32)] * 2, near=[0, 1], near_out=[0], flops=got.size * 2,
    )[0]


def decaying_sum(terms, steps, store, rows):
    for tile in range(rows // 8):
        total = terms
        while len(total) > 1:
            total = [a + b for a, b in zip(total[::2], total[1::2])]
        store(slice(tile * 8, tile * 8 + 8), total[0])
        if tile + 1 < rows // 8:
            terms = [a * b for a, b in zip(terms, steps)]


def local_kernel(first, *refs):
    sig_ref, top_ref, q_ref, edge_ref, filt_ref, fwd_ref, inv_ref, shift_ref = refs[2 * NH : 2 * NH + 8]
    conv_ref, query_ref, term_ref, step_s = refs[2 * NH + 8 : 2 * NH + 12]
    par0, par1, taps_ref, rate_s, decay_s, weight_s, sems = refs[2 * NH + 12 :]
    place = where_am_i()
    rows, group = sig_ref.shape
    modes = par0.shape[1] // 2
    step = pl.program_id(0) + first
    chip, parity = step // 2, lax.rem(step, 2)

    @pl.when(pl.program_id(0) == 0)
    def _():
        for copy in fetch_params(Mover(sems), refs[: 2 * NH], par0, par1):
            copy.wait()

    rate_s[...] = params_of(place, chip, parity, par0, par1, slice(0, modes))
    weight_s[...] = weights_of(
        rate_s[...], params_of(place, chip, parity, par0, par1, slice(modes, 2 * modes))
    )
    step_s[...] = jnp.exp(-8.0 * rate_s[...])
    decay_s[...] = jnp.exp(-rate_s[...])
    ramp = lax.broadcasted_iota(jnp.int32, (8, LANE), 0).astype(F32)

    def body(n, _):
        lanes = pl.ds(pl.multiple_of(n * LANE, LANE), LANE)
        terms = []
        for m in range(modes):
            one = slice(m, m + 1)
            terms.append(weight_s[one, lanes] * jnp.exp(-rate_s[one, lanes] * ramp))
            term_ref[8 * m : 8 * m + 8, lanes] = terms[m] * decay_s[one, lanes]

        def store(tile, value):
            taps_ref[tile, lanes] = value

        steps = [jnp.broadcast_to(step_s[m : m + 1, lanes], (8, LANE)) for m in range(modes)]
        decaying_sum(terms, steps, store, rows)
        return 0

    lax.fori_loop(0, group // LANE, body, 0)
    x = jnp.concatenate([top_ref[...], sig_ref[16:, :]], axis=0)
    th, tl = two_parts(taps_ref[...])
    sig = jnp.dot(fwd_ref[:, : 2 * rows], jnp.concatenate([x, x], axis=0), preferred_element_type=F32)
    fil = jnp.dot(fwd_ref[...], jnp.concatenate([th, th, tl], axis=0), preferred_element_type=F32)
    sr, si, fr, fi = sig[:rows], sig[rows:], fil[:rows], fil[rows:]
    ph, pw = two_parts(jnp.concatenate([sr * fr - si * fi, sr * fi + si * fr], axis=0))
    conv_ref[...] = jnp.dot(
        inv_ref[...], jnp.concatenate([ph, ph, pw], axis=0), preferred_element_type=F32
    )
    query = mix_shifted(shift_ref[...], q_ref[...], filt_ref[0])
    q0, q1 = mix_top(q_ref[0:16, :].astype(F32), edge_ref[0].astype(F32), filt_ref[0])
    query_ref[...] = top_rows(q0, q1, query).astype(BF16)


def local_call(half, pars, sig, top, q_proj, edges, filt, fwd, inv, shift):
    rows, width = q_proj.shape
    modes, group = pars[0].shape[0] // 2, pars[0].shape[1]
    par = pltpu.VMEM((NH, 2 * modes, group), F32)
    first = half * NH

    def lanes(n):
        return (0, n + first)

    def whole(array):
        return pl.BlockSpec(array.shape, lambda n: (0,) * array.ndim)

    block = pl.BlockSpec((rows, group), lambda n: (0, n))
    return pl.pallas_call(
        functools.partial(local_kernel, first),
        grid=(NH,),
        in_specs=[ANY] * (2 * NH) + [
            pl.BlockSpec((rows, group), lanes), pl.BlockSpec((16, group), lanes), pl.BlockSpec((rows, group), lanes),
            pl.BlockSpec((3, 2, group), lambda n: (0, 0, n + first)), pl.BlockSpec((3, 3, group), lambda n: (0, 0, n + first)),
            whole(fwd), whole(inv), whole(shift),
        ],
        out_specs=[block, block] + [pl.BlockSpec((count, group), lambda n: (0, n)) for count in (8 * modes, modes)],
        out_shape=[
            jax.ShapeDtypeStruct((rows, width // 2), F32),
            jax.ShapeDtypeStruct((rows, width // 2), BF16),
            jax.ShapeDtypeStruct((8 * modes, width // 2), F32),
            jax.ShapeDtypeStruct((modes, width // 2), F32),
        ],
        scratch_shapes=[par, par, pltpu.VMEM((rows, group), F32)]
        + [pltpu.VMEM((modes, group), F32)] * 3 + [pltpu.SemaphoreType.DMA((2 * NH,))],
        compiler_params=GRANT,
        cost_estimate=cost(rows * rows * group * 16 * NH),
    )(*pars, sig, top, q_proj, edges, filt, fwd, inv, shift)


def carry_kernel(state_ref, top_any, skip_any, sig_any, *refs):
    conv_anys, query_anys, term_anys, step_anys = (refs[2 * n : 2 * n + 2] for n in range(4))
    out_any, sig, top, skip, conv, query, term, step, out, state, sems = refs[8:]
    mover = Mover(sems)
    rows, width = sig.shape
    modes = step.shape[0]
    group = 512
    blocks, span = group // LANE, width // 2
    parts = [slice(at, at + group) for at in range(0, width, group)]
    fetched = []
    for at in parts:
        n, inside = at.start // span, slice(at.start % span, at.start % span + group)
        copies = [
            mover.start(anys[n].at[:, inside], here.at[:, at])
            for anys, here in ((step_anys, step), (term_anys, term), (conv_anys, conv), (query_anys, query))
        ]
        copies.append(mover.start(sig_any.at[:, at], sig.at[:, at]))
        if at.start == 0:
            copies += [mover.start(top_any, top), mover.start(skip_any, skip)]
        fetched.append(copies)
    state[...] = state_ref[...].astype(F32)
    sent = []
    for n, at in enumerate(parts):
        for copy in fetched[n]:
            copy.wait()

        def body(j, _):
            here = pl.ds(pl.multiple_of(at.start + j * LANE, LANE), LANE)
            direct = skip[:, here]
            held = []

            def store(tile, value):
                held.append(rounded(conv[tile, here] + value))
                if len(held) == 2:
                    both = slice(tile.start - 8, tile.stop)
                    signal = (top[:, here] if both.start == 0 else sig[both, here]).astype(F32)
                    total = jnp.concatenate(held, axis=0) + direct * signal
                    out[both, here] = (query[both, here].astype(F32) * total).astype(BF16)
                    held.clear()

            terms = [
                term[8 * m : 8 * m + 8, here] * state[pl.ds((n * modes + m) * blocks + j, 1), :]
                for m in range(modes)
            ]
            steps = [jnp.broadcast_to(step[m : m + 1, here], (8, LANE)) for m in range(modes)]
            decaying_sum(terms, steps, store, rows)
            return 0

        lax.fori_loop(0, blocks, body, 0)
        sent.append(mover.start(out.at[:, at], out_any.at[:, at]))
    for copy in sent:
        copy.wait()


def carry_call(states, top, skip, sig, convs, queries, terms, steps):
    rows, width = sig.shape
    half, modes = ((rows, width), BF16), steps[0].shape[0]
    return run(
        carry_kernel,
        states, top, skip, sig, *convs, *queries, *terms, *steps,
        out=[half],
        scratch=[
            half, (top.shape, BF16), (skip.shape, F32), ((rows, width), F32), half,
            ((8 * modes, width), F32), ((modes, width), F32), half, (states.shape, F32),
        ],
        near=[0],
        copies=2 + 6 * (width // 512),
        flops=rows * width * modes * 2,
    )[0]


def moved(value, target):
    return lax.ppermute(value, "ch", [(i, target(i)) for i in range(2 * NH)])


def to_chip(value, by):
    return moved(value, lambda i: (i + 2 * by) % (2 * NH))


def to_far(value):
    count, ring = lax.axis_size("seq"), 2 * NH
    pairs = [
        (s * ring + c, (s + count // 2) % count * ring + (c + NH) % ring)
        for s in range(count)
        for c in range(ring)
    ]
    return lax.ppermute(value, ("seq", "ch"), pairs)


def to_core(value):
    return moved(value, lambda i: i ^ 1)


def after(value, *others):
    return lax.optimization_barrier((value, *others))[0]


def on_device(q_proj, k_proj, v_proj, short_filter, rates, residues, skip):
    rows, width = q_proj.shape
    everyone = ("seq", "ch")
    total = lax.axis_size(everyone)
    fwd, inv = (jnp.asarray(a) for a in transforms(rows))
    shift = jnp.asarray(shifts(rows))

    own = jnp.concatenate([rates.T, residues.T], axis=0)
    far = to_far(own)
    edges = edge_call(q_proj, k_proj, v_proj)
    one = to_chip(after(own, edges), 1)
    last = lax.ppermute(edges, everyone, [(i, i + 2) for i in range(1, total - 2, 2)])
    edges = to_core(jnp.where(lax.axis_index("ch") % 2 == 1, last, edges))
    three = to_chip(own, 3)
    sig = signal_call(k_proj, v_proj, short_filter)
    mine = [own, one, far, three]
    pars = mine + [to_core(own)] + [to_core(after(value, sig)) for value in mine[1:]]
    states, top, decay, edges = state_call(pars, sig, k_proj, v_proj, edges, short_filter)

    def exchange(value):
        return lax.all_to_all(value, everyone, 0, 0, tiled=True)

    def local(half):
        return local_call(half, pars, sig, top, q_proj, edges, short_filter, fwd, inv, shift)

    got = exchange(states.reshape(total, -1, LANE)).reshape(states.shape)
    got, *early = lax.optimization_barrier((got, *local(0)))
    carry = exchange(scan_call(got, decay).reshape(total, -1, LANE)).reshape(states.shape)
    carry, *late = lax.optimization_barrier((carry, *local(1)))
    return carry_call(carry, top, skip[None, :], sig, *zip(early, late))


def solution(mesh):
    placed = (
        P(("seq", "ch"), None),
        P(("seq", "ch"), None),
        P(("seq", "ch"), None),
        P(),
        P("ch", None),
        P("ch", None),
        P(),
    )
    return jax.shard_map(
        on_device, mesh=mesh, in_specs=placed, out_specs=P(("seq", "ch"), None), check_vma=False
    )
```

```python
import functools

import jax
import jax.numpy as jnp
import numpy as np
from jax import lax
from jax.experimental import pallas as pl
from jax.experimental.pallas import tpu as pltpu
from jax.sharding import PartitionSpec as P

F32, BF16 = jnp.float32, jnp.bfloat16
NH = 4
LANE = 128
VMEM = pl.BlockSpec(memory_space=pltpu.VMEM)
ANY = pl.BlockSpec(memory_space=pl.ANY)
HBM = pl.BlockSpec(memory_space=pltpu.HBM)
GRANT = pltpu.CompilerParams(vmem_limit_bytes=60 << 20)


def two_parts(value):
    high = value.astype(BF16)
    return high, (value - high.astype(F32)).astype(BF16)


def transforms(rows):
    k = np.arange(rows)[:, None]
    n = np.arange(rows)[None, :]
    angle = np.pi * (((2 * k + 1) * n) % (4 * rows)) / (2 * rows)
    forward = np.concatenate([np.cos(angle), -np.sin(angle)], axis=0).astype(np.float32)
    inverse = (np.concatenate([np.cos(angle).T, -np.sin(angle).T], axis=1) / rows).astype(np.float32)
    bf16 = jnp.bfloat16

    def parts(array):
        high = array.astype(bf16)
        return high, (array - high.astype(np.float32)).astype(bf16)

    fh, fl = parts(forward)
    gh, gl = parts(inverse)
    return np.concatenate([fh, fl, fh], axis=1), np.concatenate([gh, gl, gh], axis=1)


def rounded(value):
    return value.astype(BF16).astype(F32)


def mix(now, one, two, taps):
    return taps[0:1] * now + taps[1:2] * one + taps[2:3] * two


def mix_top(block, edge, taps):
    a, b = block[0:1], block[1:2]
    e0, e1 = edge[0:1], edge[1:2]
    return mix(a, e1, e0, taps), mix(b, a, e1, taps)


def top_rows(first, second, rest):
    row = lax.broadcasted_iota(jnp.int32, rest.shape, 0)
    return jnp.where(row == 0, first, jnp.where(row == 1, second, rest))


def shifts(rows):
    return np.concatenate([np.roll(np.eye(rows), n, axis=0) for n in range(3)], axis=0).astype(jnp.bfloat16)


def mix_shifted(shift, block, taps):
    rows = block.shape[0]
    parts = jnp.dot(shift, block, preferred_element_type=F32)
    return mix(parts[:rows], parts[rows : 2 * rows], parts[2 * rows :], taps)


def edge_kernel(q_ref, k_ref, v_ref, edge_ref, last, sems):
    mover = Mover(sems)
    rows = q_ref.shape[0]
    copies = [
        mover.start(ref.at[rows - 16 : rows], last.at[n]) for n, ref in enumerate((q_ref, k_ref, v_ref))
    ]
    for copy in copies:
        copy.wait()
    for n in range(3):
        edge_ref[n] = last[n, 14:16, :]


def edge_call(q_proj, k_proj, v_proj):
    width = q_proj.shape[1]
    return pl.pallas_call(
        edge_kernel,
        in_specs=[ANY, ANY, ANY],
        out_specs=VMEM,
        out_shape=jax.ShapeDtypeStruct((3, 2, width), BF16),
        scratch_shapes=[pltpu.VMEM((3, 16, width), BF16), pltpu.SemaphoreType.DMA((3,))],
        compiler_params=GRANT,
        cost_estimate=cost(1 << 20),
    )(q_proj, k_proj, v_proj)


def signal_kernel(k_any, v_any, filt_any, sig_any, k, v, filt, line, sig, sems):
    mover = Mover(sems)
    rows, width = k.shape
    group = 512
    parts = [slice(at, at + group) for at in range(0, width, group)]
    small = [mover.start(filt_any.at[1:3], filt)]
    fetched = [
        (mover.start(k_any.at[:, at], k.at[:, at]), mover.start(v_any.at[:, at], v.at[:, at])) for at in parts
    ]
    for copy in small:
        copy.wait()
    line[:, 0:8, :] = jnp.zeros((4, 8, LANE), F32)

    def short(array, taps, slot, here):
        line[slot, 8:, :] = array[:, here].astype(F32)
        return mix(line[slot, 8:, :], line[slot, 7 : rows + 7, :], line[slot, 6 : rows + 6, :], taps)

    sent = []
    for at, copies in zip(parts, fetched):
        for copy in copies:
            copy.wait()
        for lane in range(at.start, at.stop, LANE):
            here = slice(lane, lane + LANE)
            slot = lane // LANE % 2 * 2
            key = short(k, filt[0, :, here], slot, here)
            value = short(v, filt[1, :, here], slot + 1, here)
            sig[:, here] = (key * value).astype(BF16)
        sent.append(mover.start(sig.at[:, at], sig_any.at[:, at]))
    for copy in sent:
        copy.wait()


def signal_call(k_proj, v_proj, filt):
    rows, width = k_proj.shape
    whole = ((rows, width), BF16)
    return run(
        signal_kernel,
        k_proj, v_proj, filt,
        out=[whole],
        scratch=[whole, whole, ((2, 3, width), F32), ((4, rows + 8, LANE), F32), whole],
        copies=1 + 3 * (width // 512),
        flops=rows * width * 12,
    )[0]


def where_am_i():
    ch = lax.axis_index("ch")
    return ch // 2, lax.rem(ch, 2), lax.axis_index("seq") * 2 * NH + ch


def cost(flops):
    return pl.CostEstimate(flops=flops, bytes_accessed=1 << 20, transcendentals=0)


def run(kernel, *operands, out, scratch=(), copies=1, flops=1 << 20, near=(), near_out=()):
    operands = [
        pltpu.with_memory_space_constraint(value, pltpu.VMEM if n in near else pltpu.HBM)
        for n, value in enumerate(operands)
    ]
    return pl.pallas_call(
        kernel,
        in_specs=[VMEM if n in near else HBM for n in range(len(operands))],
        out_specs=[VMEM if n in near_out else HBM for n in range(len(out))],
        out_shape=[
            pltpu.VMEM(*shape) if n in near_out else pltpu.HBM(*shape)
            for n, shape in enumerate(out)
        ],
        scratch_shapes=[*[pltpu.VMEM(*shape) for shape in scratch], pltpu.SemaphoreType.DMA((copies,))],
        compiler_params=pltpu.CompilerParams(vmem_limit_bytes=(24 if near or near_out else 60) << 20),
        cost_estimate=cost(flops),
    )(*operands)


class Mover:
    def __init__(self, sems):
        self.sems, self.used = sems, 0

    def start(self, source, target):
        copy = pltpu.make_async_copy(source, target, self.sems.at[self.used])
        self.used += 1
        copy.start()
        return copy


def param_at(place, chip):
    return lax.rem(place[0] + NH - chip, NH)


def params_of(place, chip, parity, par0, par1, rows):
    which = param_at(place, chip)
    return jnp.where(place[1] == parity, par0[which, rows, :], par1[which, rows, :])


def weights_of(rates, residues):
    gap = -2.0 * rates
    series = 1.0 + gap * (0.5 + gap * (1 / 6 + gap * (1 / 24 + gap * (1 / 120 + gap * (1 / 720)))))
    return residues * jnp.sqrt(-jnp.where(gap > -0.1, gap * series, jnp.exp(gap) - 1.0))


def fetch_params(mover, arrays, par0, par1):
    return [mover.start(array, par) for array, par in zip(arrays, (par0, par1))]


def states(rates, first, second, sig_ref, at):
    rows = sig_ref.shape[0]
    half = rows // 2
    decay = jnp.exp(-rates)
    early = first * decay + second
    late = sig_ref[half : half + 1, at] * decay + sig_ref[half + 1 : half + 2, at]
    for t in range(2, half):
        early = early * decay + sig_ref[t : t + 1, at]
        late = late * decay + sig_ref[half + t : half + t + 1, at]
    return early * jnp.exp(-rates * half) + late


def own_decay(place, par0, par1, span):
    modes, group = par0.shape[1] // 2, par0.shape[2]
    per_group = modes * group // (2 * LANE)
    mine = place[2]
    chip, parity = mine // (2 * per_group), lax.rem(mine // per_group, 2)
    mode, part = lax.rem(mine, per_group) // 2, lax.rem(mine, 2)
    at = pl.ds(pl.multiple_of(part * (group // 2), group // 2), group // 2)
    which = param_at(place, chip)
    rate = jnp.where(
        parity == place[1], par0[which, pl.ds(mode, 1), at], par1[which, pl.ds(mode, 1), at]
    )
    row = lax.broadcasted_iota(jnp.int32, (8, LANE), 0)
    return jnp.exp(-span * jnp.where(lax.rem(row, 2) == 0, rate[:, :LANE], rate[:, LANE:]))


def state_kernel(*refs):
    pars, (sig_any, k_any, v_any, edge, filt_any, state_out, top_any, decay, edge_any, *par_anys) = refs[: 2 * NH], refs[2 * NH : 2 * NH + 11]
    par0, par1, packed, k_top, v_top, filt, sig, top, state, sems = refs[2 * NH + 11 :]
    place = where_am_i()
    mover = Mover(sems)
    modes, group = par0.shape[1] // 2, par0.shape[2]
    width = top.shape[1]
    blocks = group // LANE
    small = [
        mover.start(filt_any.at[1:3], filt),
        mover.start(k_any.at[0:16], k_top),
        mover.start(v_any.at[0:16], v_top),
    ]
    for n, array in enumerate(pars):
        (par0, par1)[n // NH][n % NH] = array[...]
    parts = [slice(at, at + group) for at in range(0, width, group)]
    signals = [mover.start(sig_any.at[:, at], packed.at[:, at]) for at in parts]
    kept = [mover.start(a, b) for a, b in ((edge, edge_any), (par0, par_anys[0]), (par1, par_anys[1]))]
    for copy in small:
        copy.wait()
    for n, at in enumerate(parts):
        signals[n].wait()
        sig[...] = packed[:, at].astype(F32)
        key = mix_top(k_top[:, at].astype(F32), edge[1, :, at].astype(F32), filt[0, :, at])
        value = mix_top(v_top[:, at].astype(F32), edge[2, :, at].astype(F32), filt[1, :, at])
        s0, s1 = rounded(key[0] * value[0]), rounded(key[1] * value[1])
        top[:, at] = top_rows(s0, s1, sig[0:16, :]).astype(BF16)
        rates = params_of(place, n // 2, n % 2, par0, par1, slice(0, modes))
        value = states(rates, s0, s1, sig, slice(0, group))
        base = n * modes * blocks
        for j in range(blocks):
            state[pl.ds(base + j, modes, stride=blocks), :] = value[:, j * LANE : (j + 1) * LANE]
    sent = mover.start(top, top_any)
    decay[...] = own_decay(place, par0, par1, float(sig.shape[0]))
    state_out[...] = state[...].astype(BF16)
    sent.wait()
    for copy in kept:
        copy.wait()


def state_call(pars, sig, k_proj, v_proj, edges, filt):
    rows, width = k_proj.shape
    modes, group = pars[0].shape[0] // 2, pars[0].shape[1]
    par = ((NH, 2 * modes, group), F32)
    count = modes * width // LANE
    return run(
        state_kernel,
        *pars, sig, k_proj, v_proj, edges, filt,
        out=[((count, LANE), BF16), ((16, width), BF16), ((8, LANE), F32), (edges.shape, BF16), par, par],
        scratch=[
            par, par, ((rows, width), BF16), ((16, width), BF16), ((16, width), BF16),
            ((2, 3, width), F32), ((rows, group), F32), ((16, width), BF16), ((count, LANE), F32),
        ],
        near=[*range(2 * NH), 2 * NH + 3],
        near_out=[0, 2],
        copies=7 + width // group,
        flops=rows * width * modes * 2,
    )


def scan_kernel(got_ref, decay_ref, out_ref, got, sent, _):
    got[...] = got_ref[...].astype(F32)
    decay = decay_ref[0:2, :]
    total = jnp.zeros((2, LANE), F32)
    for n in range(0, got.shape[0], 2):
        sent[n : n + 2, :] = total
        total = total * decay + got[n : n + 2, :]
    out_ref[...] = sent[...].astype(BF16)


def scan_call(got, decay):
    return run(
        scan_kernel, got, decay,
        out=[(got.shape, BF16)], scratch=[(got.shape, F32)] * 2, near=[0, 1], near_out=[0], flops=got.size * 2,
    )[0]


def decaying_sum(terms, steps, store, rows):
    for tile in range(rows // 8):
        total = terms
        while len(total) > 1:
            total = [a + b for a, b in zip(total[::2], total[1::2])]
        store(slice(tile * 8, tile * 8 + 8), total[0])
        if tile + 1 < rows // 8:
            terms = [a * b for a, b in zip(terms, steps)]


def local_kernel(first, *refs):
    sig_ref, top_ref, q_ref, edge_ref, filt_ref, fwd_ref, inv_ref, shift_ref = refs[2:10]
    conv_ref, query_ref, term_ref, step_s = refs[10:14]
    par0, par1, taps_ref, rate_s, decay_s, weight_s, sems = refs[14:]
    place = where_am_i()
    rows, group = sig_ref.shape
    modes = par0.shape[1] // 2
    step = pl.program_id(0) + first
    chip, parity = step // 2, lax.rem(step, 2)

    @pl.when(pl.program_id(0) == 0)
    def _():
        for copy in fetch_params(Mover(sems), refs[:2], par0, par1):
            copy.wait()

    rate_s[...] = params_of(place, chip, parity, par0, par1, slice(0, modes))
    weight_s[...] = weights_of(
        rate_s[...], params_of(place, chip, parity, par0, par1, slice(modes, 2 * modes))
    )
    step_s[...] = jnp.exp(-8.0 * rate_s[...])
    decay_s[...] = jnp.exp(-rate_s[...])
    ramp = lax.broadcasted_iota(jnp.int32, (8, LANE), 0).astype(F32)

    def body(n, _):
        lanes = pl.ds(pl.multiple_of(n * LANE, LANE), LANE)
        terms = []
        for m in range(modes):
            one = slice(m, m + 1)
            terms.append(weight_s[one, lanes] * jnp.exp(-rate_s[one, lanes] * ramp))
            term_ref[8 * m : 8 * m + 8, lanes] = terms[m] * decay_s[one, lanes]

        def store(tile, value):
            taps_ref[tile, lanes] = value

        steps = [jnp.broadcast_to(step_s[m : m + 1, lanes], (8, LANE)) for m in range(modes)]
        decaying_sum(terms, steps, store, rows)
        return 0

    lax.fori_loop(0, group // LANE, body, 0)
    x = jnp.concatenate([top_ref[...], sig_ref[16:, :]], axis=0)
    th, tl = two_parts(taps_ref[...])
    sig = jnp.dot(fwd_ref[:, : 2 * rows], jnp.concatenate([x, x], axis=0), preferred_element_type=F32)
    fil = jnp.dot(fwd_ref[...], jnp.concatenate([th, th, tl], axis=0), preferred_element_type=F32)
    sr, si, fr, fi = sig[:rows], sig[rows:], fil[:rows], fil[rows:]
    ph, pw = two_parts(jnp.concatenate([sr * fr - si * fi, sr * fi + si * fr], axis=0))
    conv_ref[...] = jnp.dot(
        inv_ref[...], jnp.concatenate([ph, ph, pw], axis=0), preferred_element_type=F32
    )
    query = mix_shifted(shift_ref[...], q_ref[...], filt_ref[0])
    q0, q1 = mix_top(q_ref[0:16, :].astype(F32), edge_ref[0].astype(F32), filt_ref[0])
    query_ref[...] = top_rows(q0, q1, query).astype(BF16)


def local_call(half, pars, sig, top, q_proj, edges, filt, fwd, inv, shift):
    rows, width = q_proj.shape
    modes, group = pars[0].shape[1] // 2, pars[0].shape[2]
    par = pltpu.VMEM(pars[0].shape, F32)
    first = half * NH

    def lanes(n):
        return (0, n + first)

    def whole(array):
        return pl.BlockSpec(array.shape, lambda n: (0,) * array.ndim)

    block = pl.BlockSpec((rows, group), lambda n: (0, n))
    return pl.pallas_call(
        functools.partial(local_kernel, first),
        grid=(NH,),
        in_specs=[ANY] * 2 + [
            pl.BlockSpec((rows, group), lanes), pl.BlockSpec((16, group), lanes), pl.BlockSpec((rows, group), lanes),
            pl.BlockSpec((3, 2, group), lambda n: (0, 0, n + first)), pl.BlockSpec((3, 3, group), lambda n: (0, 0, n + first)),
            whole(fwd), whole(inv), whole(shift),
        ],
        out_specs=[block, block] + [pl.BlockSpec((count, group), lambda n: (0, n)) for count in (8 * modes, modes)],
        out_shape=[
            jax.ShapeDtypeStruct((rows, width // 2), F32),
            jax.ShapeDtypeStruct((rows, width // 2), BF16),
            jax.ShapeDtypeStruct((8 * modes, width // 2), F32),
            jax.ShapeDtypeStruct((modes, width // 2), F32),
        ],
        scratch_shapes=[par, par, pltpu.VMEM((rows, group), F32)]
        + [pltpu.VMEM((modes, group), F32)] * 3 + [pltpu.SemaphoreType.DMA((2,))],
        compiler_params=GRANT,
        cost_estimate=cost(rows * rows * group * 16 * NH),
    )(*pars, sig, top, q_proj, edges, filt, fwd, inv, shift)


def carry_kernel(state_ref, top_any, skip_any, sig_any, *refs):
    conv_anys, query_anys, term_anys, step_anys = (refs[2 * n : 2 * n + 2] for n in range(4))
    out_any, sig, top, skip, conv, query, term, step, out, state, sems = refs[8:]
    mover = Mover(sems)
    rows, width = sig.shape
    modes = step.shape[0]
    group = 512
    blocks, span = group // LANE, width // 2
    parts = [slice(at, at + group) for at in range(0, width, group)]
    fetched = []
    for at in parts:
        n, inside = at.start // span, slice(at.start % span, at.start % span + group)
        copies = [
            mover.start(anys[n].at[:, inside], here.at[:, at])
            for anys, here in ((step_anys, step), (term_anys, term), (conv_anys, conv), (query_anys, query))
        ]
        copies.append(mover.start(sig_any.at[:, at], sig.at[:, at]))
        if at.start == 0:
            copies += [mover.start(top_any, top), mover.start(skip_any, skip)]
        fetched.append(copies)
    state[...] = state_ref[...].astype(F32)
    sent = []
    for n, at in enumerate(parts):
        for copy in fetched[n]:
            copy.wait()

        def body(j, _):
            here = pl.ds(pl.multiple_of(at.start + j * LANE, LANE), LANE)
            direct = skip[:, here]
            held = []

            def store(tile, value):
                held.append(rounded(conv[tile, here] + value))
                if len(held) == 2:
                    both = slice(tile.start - 8, tile.stop)
                    signal = (top[:, here] if both.start == 0 else sig[both, here]).astype(F32)
                    total = jnp.concatenate(held, axis=0) + direct * signal
                    out[both, here] = (query[both, here].astype(F32) * total).astype(BF16)
                    held.clear()

            terms = [
                term[8 * m : 8 * m + 8, here] * state[pl.ds((n * modes + m) * blocks + j, 1), :]
                for m in range(modes)
            ]
            steps = [jnp.broadcast_to(step[m : m + 1, here], (8, LANE)) for m in range(modes)]
            decaying_sum(terms, steps, store, rows)
            return 0

        lax.fori_loop(0, blocks, body, 0)
        sent.append(mover.start(out.at[:, at], out_any.at[:, at]))
    for copy in sent:
        copy.wait()


def carry_call(states, top, skip, sig, convs, queries, terms, steps):
    rows, width = sig.shape
    half, modes = ((rows, width), BF16), steps[0].shape[0]
    return run(
        carry_kernel,
        states, top, skip, sig, *convs, *queries, *terms, *steps,
        out=[half],
        scratch=[
            half, (top.shape, BF16), (skip.shape, F32), ((rows, width), F32), half,
            ((8 * modes, width), F32), ((modes, width), F32), half, (states.shape, F32),
        ],
        near=[0],
        copies=2 + 6 * (width // 512),
        flops=rows * width * modes * 2,
    )[0]


def moved(value, target):
    return lax.ppermute(value, "ch", [(i, target(i)) for i in range(2 * NH)])


def to_chip(value, by):
    return moved(value, lambda i: (i + 2 * by) % (2 * NH))


def to_far(value):
    count, ring = lax.axis_size("seq"), 2 * NH
    pairs = [
        (s * ring + c, (s + count // 2) % count * ring + (c + NH) % ring)
        for s in range(count)
        for c in range(ring)
    ]
    return lax.ppermute(value, ("seq", "ch"), pairs)


def to_core(value):
    return moved(value, lambda i: i ^ 1)


def after(value, *others):
    return lax.optimization_barrier((value, *others))[0]


def on_device(q_proj, k_proj, v_proj, short_filter, rates, residues, skip):
    rows, width = q_proj.shape
    everyone = ("seq", "ch")
    total = lax.axis_size(everyone)
    fwd, inv = (jnp.asarray(a) for a in transforms(rows))
    shift = jnp.asarray(shifts(rows))

    own = jnp.concatenate([rates.T, residues.T], axis=0)
    far = to_far(own)
    edges = edge_call(q_proj, k_proj, v_proj)
    one = to_chip(after(own, edges), 1)
    last = lax.ppermute(edges, everyone, [(i, i + 2) for i in range(1, total - 2, 2)])
    edges = to_core(jnp.where(lax.axis_index("ch") % 2 == 1, last, edges))
    three = to_chip(own, 3)
    sig = signal_call(k_proj, v_proj, short_filter)
    mine = [own, one, far, three]
    pars = mine + [to_core(own)] + [to_core(after(value, sig)) for value in mine[1:]]
    states, top, decay, edges, *pars = state_call(pars, sig, k_proj, v_proj, edges, short_filter)

    def exchange(value):
        return lax.all_to_all(value, everyone, 0, 0, tiled=True)

    def local(half):
        return local_call(half, pars, sig, top, q_proj, edges, short_filter, fwd, inv, shift)

    got = exchange(states.reshape(total, -1, LANE)).reshape(states.shape)
    got, *early = lax.optimization_barrier((got, *local(0)))
    carry = exchange(scan_call(got, decay).reshape(total, -1, LANE)).reshape(states.shape)
    carry, *late = lax.optimization_barrier((carry, *local(1)))
    return carry_call(carry, top, skip[None, :], sig, *zip(early, late))


def solution(mesh):
    placed = (
        P(("seq", "ch"), None),
        P(("seq", "ch"), None),
        P(("seq", "ch"), None),
        P(),
        P("ch", None),
        P("ch", None),
        P(),
    )
    return jax.shard_map(
        on_device, mesh=mesh, in_specs=placed, out_specs=P(("seq", "ch"), None), check_vma=False
    )
```
